128 devices in a mesh: slab: 32 (over x, z, core), store: 4 (over y).
Axes of the slice: x: 4, y: 4, z: 4, core: 2. Of those that a mesh axis runs over, the one named last changes fastest.
Arguments:
- basis: bfloat16 [786432, 1024], P('slab', 'store'), may hold values from -6 to 6
- panels: bfloat16 [1024, 512], P(('slab', 'store')), may hold values from -0.1875 to 0.1875
- block_dest: int32 [2048], P(('slab', 'store')), may hold values from 0 to 2047, as said below
Outputs:
- ritz: bfloat16 [786432, 512], P(('slab', 'store'))
The draws below stay inside these ranges and needn't reach their ends.
Inputs may be any that keep to these rules, and one draw needn't show every extreme that they name: block_dest is a permutation of the row blocks. It keeps a block's index along store: block b lies in the sub-slab (b // 16) % 4 and so does block_dest[b]. The 16 blocks of one sub-slab go to 16 reader slabs, exactly 1 to each, and every reader sub-slab receives its blocks from 16 sub-slabs.
All inputs are finite; a program needn't handle non-finite values.
Results may differ from the reference program's by a relative error of at most 0.001.
Values may be sent and summed in bfloat16 or wider, within the bound.
A program may use at most 192 MiB of HBM per device.

```python
import jax
import jax.numpy as jnp

M = 1024
K = 512
BROWS = 384
BLK_DEV = 16
NBLK = 2048
NROWS = 786432
N_SLAB = 32
N_STORE = 4


def draw_block_dest(key, part):
    key = jax.random.fold_in(key, 7)
    groups = N_SLAB // 2
    per_group = BLK_DEV // groups
    first, second, third = jax.random.split(key, 3)
    offsets = jax.vmap(lambda k: jax.random.permutation(k, N_SLAB)[:groups])(jax.random.split(first, N_STORE))
    send_perm = jax.vmap(lambda k: jax.random.permutation(k, BLK_DEV))(jax.random.split(second, N_SLAB * N_STORE))
    recv_perm = jax.vmap(lambda k: jax.random.permutation(k, BLK_DEV))(jax.random.split(third, N_SLAB * N_STORE))
    send_perm = send_perm.reshape(N_SLAB, N_STORE, BLK_DEV)
    recv_perm = recv_perm.reshape(N_SLAB, N_STORE, BLK_DEV)
    slabs = jnp.broadcast_to(jnp.arange(N_SLAB, dtype=jnp.int32)[:, None, None], send_perm.shape)
    stores = jnp.broadcast_to(jnp.arange(N_STORE, dtype=jnp.int32)[None, :, None], send_perm.shape)
    group_of = send_perm // per_group
    within = send_perm % per_group
    target = (slabs + offsets[stores, group_of]) % N_SLAB
    landing = recv_perm[target, stores, group_of * per_group + within]
    dest = (target * N_STORE + stores) * BLK_DEV + landing
    return dest.reshape(NBLK).astype(jnp.int32)


def steps_of(own_key, dims, pieces, least, top_value):
    level = 1.0
    for axis_at, blocks in pieces:
        draws = jax.random.uniform(jax.random.fold_in(jax.random.fold_in(own_key, 6), axis_at), (blocks,), jnp.float32, least / len(pieces), top_value / len(pieces))
        level = level * jnp.repeat(jnp.exp(draws), dims[axis_at] // blocks).reshape((-1,) + (1,) * (len(dims) - 1 - axis_at))
    return level


def scatter_about(own_key, shape, deviation, reach, cuts=(), kind=jnp.bfloat16):
    values = jax.random.normal(own_key, shape, jnp.float32) * deviation
    if len(cuts) > 0:
        values = steps_of(own_key, shape, cuts, -0.22, 0.18) * values
    return jnp.clip(values, min=-reach, max=reach).astype(kind)


def setup_inputs(seed: int = 0) -> dict:
    keys = jax.random.split(jax.random.key(seed), 4)
    return {
        "basis": scatter_about(keys[0], (NROWS, M), 1.0, 6.0, ((0, 32), (1, 4))),
        "panels": scatter_about(keys[1], (M, K), M ** -0.5, 0.1875, ((0, 128),)),
        "block_dest": draw_block_dest(jax.random.fold_in(keys[3], 71), 0),
    }


def reference(basis, panels, block_dest):
    product = jnp.dot(basis, panels, preferred_element_type=jnp.float32).astype(jnp.bfloat16)
    blocks = product.reshape(NBLK, BROWS, K)
    placed = jnp.zeros_like(blocks).at[block_dest].set(blocks)
    return placed.reshape(NROWS, K)
```

```python
import functools

import jax
import jax.numpy as jnp
from jax import lax
from jax.experimental import pallas as pl
from jax.experimental.pallas import tpu as pltpu
from jax.sharding import PartitionSpec as P

MESH = pl.DeviceIdType.MESH

NX, NZ, NC, NY = 4, 4, 2, 4
NZC = NZ * NC
NB = 16
RR = 16
AHEAD = 4
LAG = 2


def exchange_kernel(
    basis, panels, dest, recv, table, arrived, x_out, relay, pan, pan_f32, product, pick,
    lab_out, lab_relay, lab_in, a_send, a_recv, a_local, x_send, x_recv, z_send, z_recv, z_local,
    p_send, p_recv, l_send, l_recv,
):
    rounds = arrived.shape[0]
    slab, y = lax.axis_index("slab"), lax.axis_index("store")
    x, zc = slab // NZC, slab % NZC
    z, c = zc // NC, zc % NC

    def at_y(d):
        return (slab, (y + d) % NY)

    def x_of(d):
        return (x + d) % NX

    def at_x(d):
        return (x_of(d) * NZC + zc, y)

    def zc_of(d):
        return (z + d // NC) % NZ * NC + (c + d) % NC

    def at_zc(d):
        return (x * NZC + zc_of(d), y)

    def remote(src, dst, send, received, device):
        return pltpu.make_async_remote_copy(
            src_ref=src, dst_ref=dst, send_sem=send, recv_sem=received, device_id=device, device_id_type=MESH
        )

    def wait_bytes(ref, sem):
        pltpu.make_async_copy(ref, ref, sem).wait()

    def start_basis(r):
        rows = pl.ds(pl.multiple_of(r * RR, RR), RR)
        for d in (1, 3, 2):
            remote(
                basis.at[(y + d) % NY, :, rows, :], arrived.at[r, y], a_send, a_recv.at[r], at_y(d)
            ).start()
        pltpu.make_async_copy(basis.at[y, :, rows, :], arrived.at[r, y], a_local.at[r]).start()

    barrier = pltpu.get_barrier_semaphore()
    for d in range(1, NY):
        pl.semaphore_signal(barrier, inc=1, device_id=at_y(d), device_id_type=MESH)
    for d in range(1, NX):
        pl.semaphore_signal(barrier, inc=1, device_id=at_x(d), device_id_type=MESH)
    for d in range(1, NZC):
        pl.semaphore_signal(barrier, inc=1, device_id=at_zc(d), device_id_type=MESH)
    pan_f32[y] = panels[...].astype(jnp.float32)
    pl.semaphore_wait(barrier, NY - 1 + NX - 1 + NZC - 1)

    for d in range(1, NY):
        remote(pan_f32.at[y], pan_f32.at[y], p_send.at[0], p_recv.at[0], at_y(d)).start()
    for r in range(AHEAD):
        start_basis(r)

    def choose(t, _):
        d, q = t // NZC, t % NZC
        target = x_of(d) * NZC + q
        block, place = jnp.int32(0), jnp.int32(-1)
        for b in range(NB):
            value = dest[b]
            hit = value // (NB * NY) == target
            block = jnp.where(hit, b, block)
            place = jnp.where(hit, value % NB, place)
        pick[t] = block
        lab_out[d, q] = jnp.full(lab_out.shape[2:], place, jnp.int32)
        return 0

    lax.fori_loop(0, NX * NZC, choose, 0)
    lab_relay[x] = lab_out[0]
    for d in range(1, NX):
        remote(lab_out.at[d], lab_relay.at[x], l_send.at[0], l_recv.at[0], at_x(d)).start()

    wait_bytes(pan_f32.at[pl.ds(0, NY - 1)], p_recv.at[0])
    pan[x, z, c] = pan_f32[...].reshape(pan.shape[3:]).astype(pan.dtype)
    for d in range(1, NZ):
        remote(pan.at[x, z, c], pan.at[x, z, c], p_send.at[1], p_recv.at[1], at_zc(d * NC)).start()

    wait_bytes(lab_relay.at[pl.ds(0, NX - 1)], l_recv.at[0])
    for d in range(1, NZC):
        remote(lab_relay.at[:, zc_of(d)], lab_in.at[zc], l_send.at[1], l_recv.at[1], at_zc(d)).start()
    lab_in[zc] = lab_relay[:, zc]

    wait_bytes(pan.at[0, pl.ds(0, NZ - 1), 0], p_recv.at[1])
    for d in range(1, NX):
        remote(pan.at[x, :, c], pan.at[x, :, c], p_send.at[2], p_recv.at[2], at_x(d)).start()
    wait_bytes(pan.at[pl.ds(0, NX - 1), :, 0], p_recv.at[2])
    remote(pan.at[:, :, c], pan.at[:, :, c], p_send.at[3], p_recv.at[3], at_zc(1)).start()

    wait_bytes(lab_in.at[pl.ds(0, NZC - 1)], l_recv.at[1])
    lane = lax.broadcasted_iota(jnp.int32, table.shape, 1)
    places = jnp.zeros(table.shape, jnp.int32)
    for q in range(NZC):
        for s in range(NX):
            places = jnp.where(lane == q * NX + s, lab_in[q, s], places)
    table[...] = places

    wait_bytes(pan.at[:, :, 0], p_recv.at[3])

    def one_round(r, _):
        @pl.when(r + AHEAD < rounds)
        def _():
            start_basis(r + AHEAD)

        @pl.when(r < rounds)
        def _():
            wait_bytes(arrived.at[r, pl.ds(0, NY - 1)], a_recv.at[r])
            wait_bytes(arrived.at[r, 0], a_local.at[r])
            total = None
            for s in range(NY):
                left = arrived[r, s].reshape(NB * RR, arrived.shape[-1])
                right = pan[s].reshape(arrived.shape[-1], pan.shape[-1])
                term = jnp.dot(left, right, preferred_element_type=jnp.float32)
                total = term if total is None else total + term
            product[...] = total.astype(product.dtype).reshape(product.shape)
            for d in range(1, NX):
                for q in range(NZC):
                    x_out[r, d - 1, q] = product[pick[d * NZC + q]]
                remote(x_out.at[r, d - 1], relay.at[r, x], x_send, x_recv.at[r], at_x(d)).start()
            for q in range(NZC):
                relay[r, x, q] = product[pick[q]]

        @pl.when(r >= LAG)
        def _():
            k = r - LAG
            rows = pl.ds(pl.multiple_of(k * RR, RR), RR)
            wait_bytes(relay.at[k, pl.ds(0, NX - 1)], x_recv.at[k])
            for d in range(1, NZC):
                remote(relay.at[k, :, zc_of(d)], recv.at[zc, :, rows, :], z_send, z_recv, at_zc(d)).start()
            pltpu.make_async_copy(relay.at[k, :, zc], recv.at[zc, :, rows, :], z_local).start()

        return 0

    lax.fori_loop(0, rounds + LAG, one_round, 0)

    for i in range(3):
        ref = (pan_f32.at[pl.ds(0, NY - 1)], pan.at[0, pl.ds(0, NZ - 1), 0], pan.at[pl.ds(0, NX - 1), :, 0])[i]
        wait_bytes(ref, p_send.at[i])
    wait_bytes(pan.at[:, :, 0], p_send.at[3])
    wait_bytes(lab_relay.at[pl.ds(0, NX - 1)], l_send.at[0])
    wait_bytes(lab_in.at[pl.ds(0, NZC - 1)], l_send.at[1])
    wait_bytes(arrived.at[:, pl.ds(0, NY - 1)], a_send)
    wait_bytes(x_out, x_send)
    wait_bytes(recv.at[0], z_local)
    wait_bytes(recv.at[pl.ds(0, NZC - 1)], z_send)
    wait_bytes(recv.at[pl.ds(0, NZC - 1)], z_recv)


def place_kernel(table, recv, out, held, read_sem, write_sem):
    for s in range(recv.shape[0]):
        place = table[0, s]

        @pl.when(place >= 0)
        def _():
            pltpu.make_async_copy(recv.at[s], held.at[place], read_sem.at[place]).start()

    for p in range(NB):
        pltpu.make_async_copy(recv.at[0], held.at[p], read_sem.at[p]).wait()
        pltpu.make_async_copy(held.at[p], out.at[p], write_sem.at[p]).start()
    for p in range(NB):
        pltpu.make_async_copy(held.at[p], out.at[p], write_sem.at[p]).wait()


def body(basis, panels, dest):
    depth = basis.shape[1]
    cols = panels.shape[1]
    brows = basis.shape[0] // (NY * NB)
    rounds = brows // RR
    bf16 = basis.dtype
    anywhere = pl.BlockSpec(memory_space=pl.ANY)
    vmem = pl.BlockSpec(memory_space=pltpu.VMEM)
    smem = pl.BlockSpec(memory_space=pltpu.SMEM)
    dma = pltpu.SemaphoreType.DMA
    recv, table = pl.pallas_call(
        exchange_kernel,
        out_shape=(
            jax.ShapeDtypeStruct((NZC, NX, brows, cols), bf16),
            jax.ShapeDtypeStruct((8, 128), jnp.int32),
        ),
        in_specs=[anywhere, vmem, smem],
        out_specs=(anywhere, vmem),
        scratch_shapes=[
            pltpu.VMEM((rounds, NY, NB, RR, depth), bf16),
            pltpu.VMEM((rounds, NX - 1, NZC, RR, cols), bf16),
            pltpu.VMEM((rounds, NX, NZC, RR, cols), bf16),
            pltpu.VMEM((NX, NZ, NC, NY * panels.shape[0], cols), bf16),
            pltpu.VMEM((NY, panels.shape[0], cols), jnp.float32),
            pltpu.VMEM((NB, RR, cols), bf16),
            pltpu.SMEM((NX * NZC,), jnp.int32),
            pltpu.VMEM((NX, NZC, 8, 128), jnp.int32),
            pltpu.VMEM((NX, NZC, 8, 128), jnp.int32),
            pltpu.VMEM((NZC, NX, 8, 128), jnp.int32),
            dma, dma((rounds,)), dma((rounds,)), dma, dma((rounds,)), dma, dma, dma,
            dma((4,)), dma((4,)), dma((2,)), dma((2,)),
        ],
        compiler_params=pltpu.CompilerParams(
            collective_id=0, has_side_effects=True, vmem_limit_bytes=56 * 2**20
        ),
    )(basis.reshape(NY, NB, brows, depth), panels, dest)
    out = pl.pallas_call(
        place_kernel,
        out_shape=jax.ShapeDtypeStruct((NB, brows, cols), bf16),
        in_specs=[smem, anywhere],
        out_specs=anywhere,
        scratch_shapes=[pltpu.VMEM((NB, brows, cols), bf16), dma((NB,)), dma((NB,))],
        compiler_params=pltpu.CompilerParams(vmem_limit_bytes=56 * 2**20),
    )(table, recv.reshape(NZC * NX, brows, cols))
    return out.reshape(NB * brows, cols)


def solution(mesh):
    in_specs = (P("slab", "store"), P(("slab", "store"), None), P(("slab", "store")))
    out_specs = P(("slab", "store"), None)
    return jax.shard_map(body, mesh=mesh, in_specs=in_specs, out_specs=out_specs, check_vma=False)
```

```python
import functools

import jax
import jax.numpy as jnp
from jax import lax
from jax.experimental import pallas as pl
from jax.experimental.pallas import tpu as pltpu
from jax.sharding import PartitionSpec as P

MESH = pl.DeviceIdType.MESH

NX, NZ, NC, NY = 4, 4, 2, 4
NZC = NZ * NC
NB = 16
RR = 16
AHEAD = 4
HOPS = (1, 3, 2, 0)
HERE = 6
LAG = 2


def exchange_kernel(
    basis, panels_hbm, dest_hbm, recv, table, panels, dest, arrived, x_out, relay, pan, pan_f32, product, pick,
    lab_out, lab_relay, lab_in, a_send, a_recv, a_local, x_send, x_recv, z_send, z_recv, z_local, in_sem,
    p_send, py_recv, pz_recv, px_recv, pc_recv, l_send, l_recv,
):
    rounds = arrived.shape[0]
    slab, y = lax.axis_index("slab"), lax.axis_index("store")
    x, zc = slab // NZC, slab % NZC
    z, c = zc // NC, zc % NC

    def at_y(d):
        return (slab, (y + d) % NY)

    def x_of(d):
        return (x + d) % NX

    def at_x(d):
        return (x_of(d) * NZC + zc, y)

    def zc_of(q):
        hop = HOPS[q // NC] if isinstance(q, int) else (q // NC == 0) + 3 * (q // NC == 1) + 2 * (q // NC == 2)
        return (z + hop) % NZ * NC + (c + q) % NC

    def at_zc(q):
        return (x * NZC + zc_of(q), y)

    def remote(src, dst, send, received, device):
        return pltpu.make_async_remote_copy(
            src_ref=src, dst_ref=dst, send_sem=send, recv_sem=received, device_id=device, device_id_type=MESH
        )

    def wait_bytes(ref, sem):
        pltpu.make_async_copy(ref, ref, sem).wait()

    def start_basis(r):
        rows = pl.ds(pl.multiple_of(r * RR, RR), RR)
        for d in (1, 3, 2):
            remote(
                basis.at[(y + d) % NY, :, rows, :], arrived.at[r, y], a_send, a_recv.at[r], at_y(d)
            ).start()
        pltpu.make_async_copy(basis.at[y, :, rows, :], arrived.at[r, y], a_local.at[r]).start()

    panels_in = pltpu.make_async_copy(panels_hbm, panels, in_sem.at[0])
    dest_in = pltpu.make_async_copy(dest_hbm, dest, in_sem.at[1])
    panels_in.start()
    dest_in.start()

    barrier = pltpu.get_barrier_semaphore()
    for d in range(1, NY):
        pl.semaphore_signal(barrier, inc=1, device_id=at_y(d), device_id_type=MESH)
    for d in range(1, NX):
        pl.semaphore_signal(barrier, inc=1, device_id=at_x(d), device_id_type=MESH)
    for q in range(NZC):
        if q != HERE:
            pl.semaphore_signal(barrier, inc=1, device_id=at_zc(q), device_id_type=MESH)
    panels_in.wait()
    dest_in.wait()
    pan_f32[y] = panels[...].astype(jnp.float32)
    pl.semaphore_wait(barrier, NY - 1 + NX - 1 + NZC - 1)

    for d in range(1, NY):
        remote(pan_f32.at[y], pan_f32.at[y], p_send.at[0], py_recv, at_y(d)).start()
    for r in range(AHEAD):
        start_basis(r)

    def panels_to_x(chunk):
        for d in (1, 3, 2):
            remote(chunk, chunk, p_send.at[2], px_recv.at[d], at_x(d)).start()

    def panels_to_core(chunk):
        remote(chunk, chunk, p_send.at[3], pc_recv, at_zc(HERE + 1)).start()

    wait_bytes(pan_f32.at[pl.ds(0, NY - 1)], py_recv)
    pan[x, z, c] = pan_f32[...].reshape(pan.shape[3:]).astype(pan.dtype)
    own = pan.at[x, z, c]
    for e in range(NZ - 1):
        remote(own, own, p_send.at[1], pz_recv.at[HOPS[e]], at_zc(e * NC)).start()
    panels_to_x(own)
    panels_to_core(own)
    for d in (1, 3, 2):
        wait_bytes(own, pz_recv.at[d])
        arrived_chunk = pan.at[x, (z + NZ - d) % NZ, c]
        panels_to_x(arrived_chunk)
        panels_to_core(arrived_chunk)

    def choose(t, _):
        d, q = t // NZC, t % NZC
        target = x_of(d) * NZC + zc_of(q)
        block, place = jnp.int32(0), jnp.int32(-1)
        for b in range(NB):
            value = dest[b]
            hit = value // (NB * NY) == target
            block = jnp.where(hit, b, block)
            place = jnp.where(hit, value % NB, place)
        pick[t] = block
        lab_out[d, q] = jnp.full(lab_out.shape[2:], place, jnp.int32)
        return 0

    lax.fori_loop(0, NX * NZC, choose, 0)

    for d in (1, 3, 2):
        wait_bytes(pan.at[0, :, 0], px_recv.at[d])
        panels_to_core(pan.at[x_of(NX - d), :, c])

    lab_relay[x] = lab_out[0]
    for d in range(1, NX):
        remote(lab_out.at[d], lab_relay.at[x], l_send.at[0], l_recv.at[0], at_x(d)).start()

    wait_bytes(pan.at[:, :, 0], pc_recv)

    def one_round(r, _):
        @pl.when(r + AHEAD < rounds)
        def _():
            start_basis(r + AHEAD)

        @pl.when(r < rounds)
        def _():
            wait_bytes(arrived.at[r, pl.ds(0, NY - 1)], a_recv.at[r])
            wait_bytes(arrived.at[r, 0], a_local.at[r])
            total = None
            for s in range(NY):
                left = arrived[r, s].reshape(NB * RR, arrived.shape[-1])
                right = pan[s].reshape(arrived.shape[-1], pan.shape[-1])
                term = jnp.dot(left, right, preferred_element_type=jnp.float32)
                total = term if total is None else total + term
            product[...] = total.astype(product.dtype).reshape(product.shape)
            for d in range(1, NX):
                for q in range(NZC):
                    x_out[r, d - 1, q] = product[pick[d * NZC + q]]
            for h in range(NZ):
                half = pl.ds(h * NC, NC)
                for d in range(1, NX):
                    remote(
                        x_out.at[r, d - 1, half], relay.at[r, x, half], x_send, x_recv.at[r, h], at_x(d)
                    ).start()
            for q in range(NZC):
                relay[r, x, q] = product[pick[q]]

        @pl.when(r >= LAG)
        def _():
            k = r - LAG
            rows = pl.ds(pl.multiple_of(k * RR, RR), RR)
            for h in range(NZ):
                wait_bytes(relay.at[k, pl.ds(0, NX - 1), pl.ds(0, NC)], x_recv.at[k, h])
                for q in range(h * NC, (h + 1) * NC):
                    if q == HERE:
                        pltpu.make_async_copy(relay.at[k, :, q], recv.at[zc, :, rows, :], z_local).start()
                    else:
                        remote(relay.at[k, :, q], recv.at[zc, :, rows, :], z_send, z_recv, at_zc(q)).start()

        @pl.when(r == 1)
        def _():
            wait_bytes(lab_relay.at[pl.ds(0, NX - 1)], l_recv.at[0])
            for q in range(NZC):
                if q != HERE:
                    remote(lab_relay.at[:, q], lab_in.at[zc], l_send.at[1], l_recv.at[1], at_zc(q)).start()
            lab_in[zc] = lab_relay[:, HERE]

        @pl.when(r == 3)
        def _():
            wait_bytes(lab_in.at[pl.ds(0, NZC - 1)], l_recv.at[1])
            lane = lax.broadcasted_iota(jnp.int32, table.shape, 1)
            places = jnp.zeros(table.shape, jnp.int32)
            for q in range(NZC):
                for s in range(NX):
                    places = jnp.where(lane == q * NX + s, lab_in[q, s], places)
            table[...] = places

        return 0

    lax.fori_loop(0, rounds + LAG, one_round, 0)

    wait_bytes(pan_f32.at[pl.ds(0, NY - 1)], p_send.at[0])
    wait_bytes(pan.at[0, pl.ds(0, NZ - 1), 0], p_send.at[1])
    wait_bytes(pan.at[pl.ds(0, NX - 1), :, 0], p_send.at[2])
    wait_bytes(pan.at[:, :, 0], p_send.at[3])
    wait_bytes(lab_relay.at[pl.ds(0, NX - 1)], l_send.at[0])
    wait_bytes(lab_in.at[pl.ds(0, NZC - 1)], l_send.at[1])
    wait_bytes(arrived.at[:, pl.ds(0, NY - 1)], a_send)
    wait_bytes(x_out, x_send)
    wait_bytes(recv.at[0], z_local)
    wait_bytes(recv.at[pl.ds(0, NZC - 1)], z_send)
    wait_bytes(recv.at[pl.ds(0, NZC - 1)], z_recv)


def place_kernel(table, recv, out, sem):
    for s in range(recv.shape[0]):
        place = table[0, s]

        @pl.when(place >= 0)
        def _():
            pltpu.make_async_copy(recv.at[s], out.at[place], sem.at[place]).start()

    for p in range(NB):
        pltpu.make_async_copy(recv.at[0], out.at[p], sem.at[p]).wait()


def body(basis, panels, dest):
    depth = basis.shape[1]
    cols = panels.shape[1]
    brows = basis.shape[0] // (NY * NB)
    rounds = brows // RR
    bf16 = basis.dtype
    anywhere = pl.BlockSpec(memory_space=pl.ANY)
    vmem = pl.BlockSpec(memory_space=pltpu.VMEM)
    smem = pl.BlockSpec(memory_space=pltpu.SMEM)
    in_hbm = pl.BlockSpec(memory_space=pltpu.HBM)
    dma = pltpu.SemaphoreType.DMA
    recv, table = pl.pallas_call(
        exchange_kernel,
        out_shape=(
            jax.ShapeDtypeStruct((NZC, NX, brows, cols), bf16),
            jax.ShapeDtypeStruct((8, 128), jnp.int32),
        ),
        in_specs=[anywhere, in_hbm, in_hbm],
        out_specs=(anywhere, vmem),
        scratch_shapes=[
            pltpu.VMEM(panels.shape, bf16),
            pltpu.SMEM(dest.shape, jnp.int32),
            pltpu.VMEM((rounds, NY, NB, RR, depth), bf16),
            pltpu.VMEM((rounds, NX - 1, NZC, RR, cols), bf16),
            pltpu.VMEM((rounds, NX, NZC, RR, cols), bf16),
            pltpu.VMEM((NX, NZ, NC, NY * panels.shape[0], cols), bf16),
            pltpu.VMEM((NY, panels.shape[0], cols), jnp.float32),
            pltpu.VMEM((NB, RR, cols), bf16),
            pltpu.SMEM((NX * NZC,), jnp.int32),
            pltpu.VMEM((NX, NZC, 8, 128), jnp.int32),
            pltpu.VMEM((NX, NZC, 8, 128), jnp.int32),
            pltpu.VMEM((NZC, NX, 8, 128), jnp.int32),
            dma, dma((rounds,)), dma((rounds,)), dma, dma((rounds, NZ)), dma, dma, dma, dma((2,)),
            dma((4,)), dma, dma((NZ,)), dma((NX,)), dma, dma((2,)), dma((2,)),
        ],
        compiler_params=pltpu.CompilerParams(
            collective_id=0, has_side_effects=True, vmem_limit_bytes=40 * 2**20
        ),
    )(basis.reshape(NY, NB, brows, depth), panels, dest)
    out = pl.pallas_call(
        place_kernel,
        out_shape=jax.ShapeDtypeStruct((NB, brows, cols), bf16),
        in_specs=[smem, anywhere],
        out_specs=anywhere,
        scratch_shapes=[dma((NB,))],
        compiler_params=pltpu.CompilerParams(vmem_limit_bytes=2 * 2**20),
    )(table, recv.reshape(NZC * NX, brows, cols))
    return out.reshape(NB * brows, cols)


def solution(mesh):
    in_specs = (P("slab", "store"), P(("slab", "store"), None), P(("slab", "store")))
    out_specs = P(("slab", "store"), None)
    return jax.shard_map(body, mesh=mesh, in_specs=in_specs, out_specs=out_specs, check_vma=False)
```

```python
import functools

import jax
import jax.numpy as jnp
from jax import lax
from jax.experimental import pallas as pl
from jax.experimental.pallas import tpu as pltpu
from jax.sharding import PartitionSpec as P

MESH = pl.DeviceIdType.MESH

NX, NZ, NC, NY = 4, 4, 2, 4
NZC = NZ * NC
NB = 16
RR = 16
AHEAD = 4
HOPS = (1, 3, 2, 0)
HERE = 6
NG = 2


def exchange_kernel(
    basis, panels_hbm, dest_hbm, recv, table, panels, dest, arrived, x_out, relay, pan, pan_f32, product, pick,
    lab_out, lab_relay, lab_in, a_send, a_recv, a_local, x_send, x_recv, z_send, z_recv, z_local, in_sem,
    p_send, py_recv, p_recv, pc_recv, l_send, l_recv,
):
    rounds = arrived.shape[0]
    slab, y = lax.axis_index("slab"), lax.axis_index("store")
    x, zc = slab // NZC, slab % NZC
    z, c = zc // NC, zc % NC

    def at_y(d):
        return (slab, (y + d) % NY)

    def x_of(d):
        return (x + d) % NX

    def at_x(d):
        return (x_of(d) * NZC + zc, y)

    def zc_of(q):
        hop = HOPS[q // NC] if isinstance(q, int) else (q // NC == 0) + 3 * (q // NC == 1) + 2 * (q // NC == 2)
        return (z + hop) % NZ * NC + (c + q) % NC

    def at_zc(q):
        return (x * NZC + zc_of(q), y)

    def at_xz(d, e):
        return (x_of(d) * NZC + zc_of(e * NC), y)

    def remote(src, dst, send, received, device):
        return pltpu.make_async_remote_copy(
            src_ref=src, dst_ref=dst, send_sem=send, recv_sem=received, device_id=device, device_id_type=MESH
        )

    def wait_bytes(ref, sem):
        pltpu.make_async_copy(ref, ref, sem).wait()

    def start_basis(r):
        rows = pl.ds(pl.multiple_of(r * RR, RR), RR)
        for d in (1, 3, 2):
            remote(
                basis.at[(y + d) % NY, :, rows, :], arrived.at[r, y], a_send, a_recv.at[r], at_y(d)
            ).start()
        pltpu.make_async_copy(basis.at[y, :, rows, :], arrived.at[r, y], a_local.at[r]).start()

    panels_in = pltpu.make_async_copy(panels_hbm, panels, in_sem.at[0])
    dest_in = pltpu.make_async_copy(dest_hbm, dest, in_sem.at[1])
    panels_in.start()
    dest_in.start()

    barrier = pltpu.get_barrier_semaphore()
    for d in range(1, NY):
        pl.semaphore_signal(barrier, inc=1, device_id=at_y(d), device_id_type=MESH)
    for d in range(1, NX):
        pl.semaphore_signal(barrier, inc=1, device_id=at_x(d), device_id_type=MESH)
    for d in range(1, NX):
        for e in range(NZ - 1):
            pl.semaphore_signal(barrier, inc=1, device_id=at_xz(d, e), device_id_type=MESH)
    for q in range(NZC):
        if q != HERE:
            pl.semaphore_signal(barrier, inc=1, device_id=at_zc(q), device_id_type=MESH)
    panels_in.wait()
    dest_in.wait()
    pan_f32[y] = panels[...].astype(jnp.float32)
    pl.semaphore_wait(barrier, NY - 1 + NX - 1 + (NX - 1) * (NZ - 1) + NZC - 1)

    for d in range(1, NY):
        remote(pan_f32.at[y], pan_f32.at[y], p_send.at[0, 0], py_recv, at_y(d)).start()
    for r in range(AHEAD):
        start_basis(r)

    width = pan.shape[-1]
    wait_bytes(pan_f32.at[pl.ds(0, NY - 1)], py_recv)
    for g in range(NG):
        part = pan_f32[:, :, g * width : (g + 1) * width]
        pan[g, x, z, c] = part.reshape(pan.shape[4:]).astype(pan.dtype)
        own = pan.at[g, x, z, c]
        for d in (2, 1, 3):
            for e in (2, 0, 1):
                remote(own, own, p_send.at[1, g], p_recv.at[0, g], at_xz(d, e)).start()
            remote(own, own, p_send.at[2, g], p_recv.at[1, g], at_x(d)).start()
        for e in (2, 0, 1):
            remote(own, own, p_send.at[3, g], p_recv.at[2, g], at_zc(e * NC)).start()

    def panels_in_line(g):
        wait_bytes(pan.at[g, pl.ds(0, NX - 1), pl.ds(0, NZ - 1), 0], p_recv.at[0, g])
        wait_bytes(pan.at[g, pl.ds(0, NX - 1), 0, 0], p_recv.at[1, g])
        wait_bytes(pan.at[g, 0, pl.ds(0, NZ - 1), 0], p_recv.at[2, g])
        half = pan.at[g, :, :, c]
        remote(half, half, p_send.at[4, g], pc_recv.at[g], at_zc(HERE + 1)).start()

    def choose(t, _):
        d, q = t // NZC, t % NZC
        target = x_of(d) * NZC + zc_of(q)
        block, place = jnp.int32(0), jnp.int32(-1)
        for b in range(NB):
            value = dest[b]
            hit = value // (NB * NY) == target
            block = jnp.where(hit, b, block)
            place = jnp.where(hit, value % NB, place)
        pick[t] = block
        lab_out[d, q] = jnp.full(lab_out.shape[2:], place, jnp.int32)
        return 0

    lax.fori_loop(0, NX * NZC, choose, 0)

    panels_in_line(0)
    lab_relay[x] = lab_out[0]
    for d in range(1, NX):
        remote(lab_out.at[d], lab_relay.at[x], l_send.at[0], l_recv.at[0], at_x(d)).start()

    panels_in_line(1)
    wait_bytes(pan.at[0, :, :, 0], pc_recv.at[0])

    def forward(r, g, h):
        rows, columns = pl.ds(pl.multiple_of(r * RR, RR), RR), pl.ds(g * width, width)
        wait_bytes(relay.at[r, g, pl.ds(0, NX - 1), pl.ds(0, NZC // 2)], x_recv.at[r, g, h])
        for q in range(h * (NZC // 2), (h + 1) * (NZC // 2)):
            src, dst = relay.at[r, g, :, q], recv.at[zc, :, rows, columns]
            if q == HERE:
                pltpu.make_async_copy(src, dst, z_local).start()
            else:
                remote(src, dst, z_send, z_recv, at_zc(q)).start()

    def one_round(r, _):
        @pl.when(r + AHEAD < rounds)
        def _():
            start_basis(r + AHEAD)

        @pl.when(r < rounds)
        def _():
            wait_bytes(arrived.at[r, pl.ds(0, NY - 1)], a_recv.at[r])
            wait_bytes(arrived.at[r, 0], a_local.at[r])
            for g in range(NG):
                if g == 1:

                    @pl.when(r == 0)
                    def _():
                        wait_bytes(pan.at[1, :, :, 0], pc_recv.at[1])

                total = None
                for s in range(NY):
                    left = arrived[r, s].reshape(NB * RR, arrived.shape[-1])
                    right = pan[g, s].reshape(arrived.shape[-1], width)
                    term = jnp.dot(left, right, preferred_element_type=jnp.float32)
                    total = term if total is None else total + term
                product[...] = total.astype(product.dtype).reshape(product.shape)
                for d in range(1, NX):
                    for q in range(NZC):
                        x_out[r, g, d - 1, q] = product[pick[d * NZC + q]]
                for h in range(2):
                    half = pl.ds(h * (NZC // 2), NZC // 2)
                    for d in (1, 3, 2):
                        remote(
                            x_out.at[r, g, d - 1, half], relay.at[r, g, x, half], x_send, x_recv.at[r, g, h], at_x(d)
                        ).start()
                for q in range(NZC):
                    relay[r, g, x, q] = product[pick[q]]

        @pl.when(r >= 1)
        def _():
            for g, h in ((0, 1), (1, 0), (1, 1)):
                forward(r - 1, g, h)

        @pl.when(r < rounds)
        def _():
            forward(r, 0, 0)

        @pl.when(r == 1)
        def _():
            wait_bytes(lab_relay.at[pl.ds(0, NX - 1)], l_recv.at[0])
            for q in range(NZC):
                if q != HERE:
                    remote(lab_relay.at[:, q], lab_in.at[zc], l_send.at[1], l_recv.at[1], at_zc(q)).start()
            lab_in[zc] = lab_relay[:, HERE]

        @pl.when(r == 3)
        def _():
            wait_bytes(lab_in.at[pl.ds(0, NZC - 1)], l_recv.at[1])
            lane = lax.broadcasted_iota(jnp.int32, table.shape, 1)
            places = jnp.zeros(table.shape, jnp.int32)
            for q in range(NZC):
                for s in range(NX):
                    places = jnp.where(lane == q * NX + s, lab_in[q, s], places)
            table[...] = places

        return 0

    lax.fori_loop(0, rounds + 1, one_round, 0)

    wait_bytes(pan_f32.at[pl.ds(0, NY - 1)], p_send.at[0, 0])
    for g in range(NG):
        wait_bytes(pan.at[g, pl.ds(0, NX - 1), pl.ds(0, NZ - 1), 0], p_send.at[1, g])
        wait_bytes(pan.at[g, pl.ds(0, NX - 1), 0, 0], p_send.at[2, g])
        wait_bytes(pan.at[g, 0, pl.ds(0, NZ - 1), 0], p_send.at[3, g])
        wait_bytes(pan.at[g, :, :, 0], p_send.at[4, g])
    wait_bytes(lab_relay.at[pl.ds(0, NX - 1)], l_send.at[0])
    wait_bytes(lab_in.at[pl.ds(0, NZC - 1)], l_send.at[1])
    wait_bytes(arrived.at[:, pl.ds(0, NY - 1)], a_send)
    wait_bytes(x_out, x_send)
    wait_bytes(recv.at[0], z_local)
    wait_bytes(recv.at[pl.ds(0, NZC - 1)], z_send)
    wait_bytes(recv.at[pl.ds(0, NZC - 1)], z_recv)


def place_kernel(table, recv, out, sem):
    for s in range(recv.shape[0]):
        place = table[0, s]

        @pl.when(place >= 0)
        def _():
            pltpu.make_async_copy(recv.at[s], out.at[place], sem.at[place]).start()

    for p in range(NB):
        pltpu.make_async_copy(recv.at[0], out.at[p], sem.at[p]).wait()


def body(basis, panels, dest):
    depth = basis.shape[1]
    cols = panels.shape[1]
    brows = basis.shape[0] // (NY * NB)
    rounds = brows // RR
    bf16 = basis.dtype
    anywhere = pl.BlockSpec(memory_space=pl.ANY)
    vmem = pl.BlockSpec(memory_space=pltpu.VMEM)
    smem = pl.BlockSpec(memory_space=pltpu.SMEM)
    in_hbm = pl.BlockSpec(memory_space=pltpu.HBM)
    hbm = lambda a: pltpu.with_memory_space_constraint(a, pltpu.HBM)
    dma = pltpu.SemaphoreType.DMA
    recv, table = pl.pallas_call(
        exchange_kernel,
        out_shape=(
            jax.ShapeDtypeStruct((NZC, NX, brows, cols), bf16),
            jax.ShapeDtypeStruct((8, 128), jnp.int32),
        ),
        in_specs=[anywhere, in_hbm, in_hbm],
        out_specs=(anywhere, vmem),
        scratch_shapes=[
            pltpu.VMEM(panels.shape, bf16),
            pltpu.SMEM(dest.shape, jnp.int32),
            pltpu.VMEM((rounds, NY, NB, RR, depth), bf16),
            pltpu.VMEM((rounds, NG, NX - 1, NZC, RR, cols // NG), bf16),
            pltpu.VMEM((rounds, NG, NX, NZC, RR, cols // NG), bf16),
            pltpu.VMEM((NG, NX, NZ, NC, NY * panels.shape[0], cols // NG), bf16),
            pltpu.VMEM((NY, panels.shape[0], cols), jnp.float32),
            pltpu.VMEM((NB, RR, cols // NG), bf16),
            pltpu.SMEM((NX * NZC,), jnp.int32),
            pltpu.VMEM((NX, NZC, 8, 128), jnp.int32),
            pltpu.VMEM((NX, NZC, 8, 128), jnp.int32),
            pltpu.VMEM((NZC, NX, 8, 128), jnp.int32),
            dma, dma((rounds,)), dma((rounds,)), dma, dma((rounds, NG, 2)), dma, dma, dma, dma((2,)),
            dma((5, NG)), dma, dma((3, NG)), dma((NG,)), dma((2,)), dma((2,)),
        ],
        compiler_params=pltpu.CompilerParams(
            collective_id=0, has_side_effects=True, vmem_limit_bytes=40 * 2**20
        ),
    )(basis.reshape(NY, NB, brows, depth), hbm(panels), hbm(dest))
    out = pl.pallas_call(
        place_kernel,
        out_shape=jax.ShapeDtypeStruct((NB, brows, cols), bf16),
        in_specs=[smem, anywhere],
        out_specs=anywhere,
        scratch_shapes=[dma((NB,))],
        compiler_params=pltpu.CompilerParams(vmem_limit_bytes=2 * 2**20),
    )(table, recv.reshape(NZC * NX, brows, cols))
    return out.reshape(NB * brows, cols)


def solution(mesh):
    in_specs = (P("slab", "store"), P(("slab", "store"), None), P(("slab", "store")))
    out_specs = P(("slab", "store"), None)
    return jax.shard_map(body, mesh=mesh, in_specs=in_specs, out_specs=out_specs, check_vma=False)
```

```python
import functools

import jax
import jax.numpy as jnp
from jax import lax
from jax.experimental import pallas as pl
from jax.experimental.pallas import tpu as pltpu
from jax.sharding import PartitionSpec as P

MESH = pl.DeviceIdType.MESH

NX, NZ, NC, NY = 4, 4, 2, 4
NZC = NZ * NC
NB = 16
RR = 16
AHEAD = 4
HOPS = (1, 3, 2, 0)
HERE = 6
SENT = (0, 1, 2, 3, 4, 5, 7)
NG = 4


def exchange_kernel(
    basis, panels_hbm, dest_hbm, recv, table, panels, dest, arrived, x_out, x_relay, z_out, z_relay, pan, pan_f32, product, pick,
    lab_out, lab_relay, lab_in, a_send, a_recv, a_local, x_send, x_recv, z_send, z_recv, z2_send, z2_recv, x2_send, x2_recv, local, in_sem,
    p_send, py_recv, p_recv, pc_recv, l_send, l_recv,
):
    rounds = arrived.shape[0]
    slab, y = lax.axis_index("slab"), lax.axis_index("store")
    x, zc = slab // NZC, slab % NZC
    z, c = zc // NC, zc % NC

    def at_y(d):
        return (slab, (y + d) % NY)

    def x_of(d):
        return (x + d) % NX

    def at_x(d):
        return (x_of(d) * NZC + zc, y)

    def zc_of(q):
        hop = HOPS[q // NC] if isinstance(q, int) else (q // NC == 0) + 3 * (q // NC == 1) + 2 * (q // NC == 2)
        return (z + hop) % NZ * NC + (c + q) % NC

    def at_zc(q):
        return (x * NZC + zc_of(q), y)

    def at_xz(d, e):
        return (x_of(d) * NZC + zc_of(e * NC), y)

    def remote(src, dst, send, received, device):
        return pltpu.make_async_remote_copy(
            src_ref=src, dst_ref=dst, send_sem=send, recv_sem=received, device_id=device, device_id_type=MESH
        )

    def wait_bytes(ref, sem):
        pltpu.make_async_copy(ref, ref, sem).wait()

    def start_basis(r):
        rows = pl.ds(pl.multiple_of(r * RR, RR), RR)
        for d in (1, 3, 2):
            remote(
                basis.at[(y + d) % NY, :, rows, :], arrived.at[r, y], a_send, a_recv.at[r], at_y(d)
            ).start()
        pltpu.make_async_copy(basis.at[y, :, rows, :], arrived.at[r, y], a_local.at[r]).start()

    panels_in = pltpu.make_async_copy(panels_hbm, panels, in_sem.at[0])
    dest_in = pltpu.make_async_copy(dest_hbm, dest, in_sem.at[1])
    panels_in.start()
    dest_in.start()

    barrier = pltpu.get_barrier_semaphore()
    for d in range(1, NY):
        pl.semaphore_signal(barrier, inc=1, device_id=at_y(d), device_id_type=MESH)
    for d in range(1, NX):
        pl.semaphore_signal(barrier, inc=1, device_id=at_x(d), device_id_type=MESH)
    for d in range(1, NX):
        for e in range(NZ - 1):
            pl.semaphore_signal(barrier, inc=1, device_id=at_xz(d, e), device_id_type=MESH)
    for q in range(NZC):
        if q != HERE:
            pl.semaphore_signal(barrier, inc=1, device_id=at_zc(q), device_id_type=MESH)
    panels_in.wait()
    dest_in.wait()
    pan_f32[y] = panels[...].astype(jnp.float32)
    pl.semaphore_wait(barrier, NY - 1 + NX - 1 + (NX - 1) * (NZ - 1) + NZC - 1)

    for d in range(1, NY):
        remote(pan_f32.at[y], pan_f32.at[y], p_send.at[0, 0], py_recv, at_y(d)).start()
    for r in range(AHEAD):
        start_basis(r)

    width = pan.shape[-1]
    wait_bytes(pan_f32.at[pl.ds(0, NY - 1)], py_recv)
    for g in range(NG):
        part = pan_f32[:, :, g * width : (g + 1) * width]
        pan[g, x, z, c] = part.reshape(pan.shape[4:]).astype(pan.dtype)
        own = pan.at[g, x, z, c]
        for d in (2, 1, 3):
            for e in (2, 0, 1):
                remote(own, own, p_send.at[1, g], p_recv.at[0, g], at_xz(d, e)).start()
            remote(own, own, p_send.at[2, g], p_recv.at[1, g], at_x(d)).start()
        for e in (2, 0, 1):
            remote(own, own, p_send.at[3, g], p_recv.at[2, g], at_zc(e * NC)).start()

    def panels_in_line(g):
        wait_bytes(pan.at[g, pl.ds(0, NX - 1), pl.ds(0, NZ - 1), 0], p_recv.at[0, g])
        wait_bytes(pan.at[g, pl.ds(0, NX - 1), 0, 0], p_recv.at[1, g])
        wait_bytes(pan.at[g, 0, pl.ds(0, NZ - 1), 0], p_recv.at[2, g])
        half = pan.at[g, :, :, c]
        remote(half, half, p_send.at[4, g], pc_recv.at[g], at_zc(HERE + 1)).start()

    def choose(t, _):
        d, q = t // NZC, t % NZC
        target = x_of(d) * NZC + zc_of(q)
        block, place = jnp.int32(0), jnp.int32(-1)
        for b in range(NB):
            value = dest[b]
            hit = value // (NB * NY) == target
            block = jnp.where(hit, b, block)
            place = jnp.where(hit, value % NB, place)
        pick[t] = block
        lab_out[d, q] = jnp.full(lab_out.shape[2:], place, jnp.int32)
        return 0

    lax.fori_loop(0, NX * NZC, choose, 0)

    panels_in_line(0)
    lab_relay[x] = lab_out[0]
    for d in range(1, NX):
        remote(lab_out.at[d], lab_relay.at[x], l_send.at[0], l_recv.at[0], at_x(d)).start()

    def forward(r, g):
        rows, columns = pl.ds(pl.multiple_of(r * RR, RR), RR), pl.ds(g * width, width)
        k = g // 2
        if g % 2 == 0:
            wait_bytes(x_relay.at[r, k, pl.ds(0, NX - 1)], x_recv.at[r, k])
            dst = recv.at[zc, :, rows, columns]
            for q in SENT:
                remote(x_relay.at[r, k, :, q], dst, z2_send, z2_recv, at_zc(q)).start()
            pltpu.make_async_copy(x_relay.at[r, k, :, HERE], dst, local.at[0]).start()
        else:
            wait_bytes(z_relay.at[r, k, pl.ds(0, NZC - 1)], z_recv.at[r, k])
            dst = recv.at[:, x, rows, columns]
            for d in (1, 3, 2):
                remote(z_relay.at[r, k, :, d], dst, x2_send, x2_recv, at_x(d)).start()
            pltpu.make_async_copy(z_relay.at[r, k, :, 0], dst, local.at[1]).start()

    def one_round(r, _):
        @pl.when(r + AHEAD < rounds)
        def _():
            start_basis(r + AHEAD)

        @pl.when(r < rounds)
        def _():
            wait_bytes(arrived.at[r, pl.ds(0, NY - 1)], a_recv.at[r])
            wait_bytes(arrived.at[r, 0], a_local.at[r])
            for g in range(NG):
                @pl.when(r == 0)
                def _():
                    if g + 1 < NG:
                        panels_in_line(g + 1)
                    wait_bytes(pan.at[g, :, :, 0], pc_recv.at[g])

                total = None
                for s in range(NY):
                    left = arrived[r, s].reshape(NB * RR, arrived.shape[-1])
                    right = pan[g, s].reshape(arrived.shape[-1], width)
                    term = jnp.dot(left, right, preferred_element_type=jnp.float32)
                    total = term if total is None else total + term
                product[...] = total.astype(product.dtype).reshape(product.shape)
                k = g // 2
                if g % 2 == 0:
                    for d in range(1, NX):
                        for q in range(NZC):
                            x_out[r, k, d - 1, q] = product[pick[d * NZC + q]]
                    for d in (1, 3, 2):
                        remote(
                            x_out.at[r, k, d - 1], x_relay.at[r, k, x], x_send, x_recv.at[r, k], at_x(d)
                        ).start()
                    for q in range(NZC):
                        x_relay[r, k, x, q] = product[pick[q]]
                else:
                    for q in range(NZC):
                        for d in range(NX):
                            if q == HERE:
                                z_relay[r, k, zc, d] = product[pick[d * NZC + q]]
                            else:
                                z_out[r, k, SENT.index(q), d] = product[pick[d * NZC + q]]
                    for i, q in enumerate(SENT):
                        remote(
                            z_out.at[r, k, i], z_relay.at[r, k, zc], z_send, z_recv.at[r, k], at_zc(q)
                        ).start()

        @pl.when(r >= 1)
        def _():
            for g in range(NG):
                forward(r - 1, g)

        @pl.when(r == 1)
        def _():
            wait_bytes(lab_relay.at[pl.ds(0, NX - 1)], l_recv.at[0])
            for q in range(NZC):
                if q != HERE:
                    remote(lab_relay.at[:, q], lab_in.at[zc], l_send.at[1], l_recv.at[1], at_zc(q)).start()
            lab_in[zc] = lab_relay[:, HERE]

        @pl.when(r == 3)
        def _():
            wait_bytes(lab_in.at[pl.ds(0, NZC - 1)], l_recv.at[1])
            lane = lax.broadcasted_iota(jnp.int32, table.shape, 1)
            places = jnp.zeros(table.shape, jnp.int32)
            for q in range(NZC):
                for s in range(NX):
                    places = jnp.where(lane == q * NX + s, lab_in[q, s], places)
            table[...] = places

        return 0

    lax.fori_loop(0, rounds + 1, one_round, 0)

    wait_bytes(pan_f32.at[pl.ds(0, NY - 1)], p_send.at[0, 0])
    for g in range(NG):
        wait_bytes(pan.at[g, pl.ds(0, NX - 1), pl.ds(0, NZ - 1), 0], p_send.at[1, g])
        wait_bytes(pan.at[g, pl.ds(0, NX - 1), 0, 0], p_send.at[2, g])
        wait_bytes(pan.at[g, 0, pl.ds(0, NZ - 1), 0], p_send.at[3, g])
        wait_bytes(pan.at[g, :, :, 0], p_send.at[4, g])
    wait_bytes(lab_relay.at[pl.ds(0, NX - 1)], l_send.at[0])
    wait_bytes(lab_in.at[pl.ds(0, NZC - 1)], l_send.at[1])
    wait_bytes(arrived.at[:, pl.ds(0, NY - 1)], a_send)
    wait_bytes(x_out, x_send)
    half = pl.ds(0, NG // 2 * width)
    wait_bytes(z_out, z_send)
    wait_bytes(recv.at[0, :, :, half], local.at[0])
    wait_bytes(recv.at[:, 0, :, half], local.at[1])
    wait_bytes(recv.at[pl.ds(0, NZC - 1), :, :, half], z2_send)
    wait_bytes(recv.at[:, pl.ds(0, NX - 1), :, half], x2_send)
    wait_bytes(recv.at[pl.ds(0, NZC - 1), :, :, half], z2_recv)
    wait_bytes(recv.at[:, pl.ds(0, NX - 1), :, half], x2_recv)


def place_kernel(table, recv, out, sem):
    for s in range(recv.shape[0]):
        place = table[0, s]

        @pl.when(place >= 0)
        def _():
            pltpu.make_async_copy(recv.at[s], out.at[place], sem.at[place]).start()

    for p in range(NB):
        pltpu.make_async_copy(recv.at[0], out.at[p], sem.at[p]).wait()


def body(basis, panels, dest):
    depth = basis.shape[1]
    cols = panels.shape[1]
    brows = basis.shape[0] // (NY * NB)
    rounds = brows // RR
    bf16 = basis.dtype
    anywhere = pl.BlockSpec(memory_space=pl.ANY)
    vmem = pl.BlockSpec(memory_space=pltpu.VMEM)
    smem = pl.BlockSpec(memory_space=pltpu.SMEM)
    in_hbm = pl.BlockSpec(memory_space=pltpu.HBM)
    hbm = lambda a: pltpu.with_memory_space_constraint(a, pltpu.HBM)
    dma = pltpu.SemaphoreType.DMA
    recv, table = pl.pallas_call(
        exchange_kernel,
        out_shape=(
            jax.ShapeDtypeStruct((NZC, NX, brows, cols), bf16),
            jax.ShapeDtypeStruct((8, 128), jnp.int32),
        ),
        in_specs=[anywhere, in_hbm, in_hbm],
        out_specs=(anywhere, vmem),
        scratch_shapes=[
            pltpu.VMEM(panels.shape, bf16),
            pltpu.SMEM(dest.shape, jnp.int32),
            pltpu.VMEM((rounds, NY, NB, RR, depth), bf16),
            pltpu.VMEM((rounds, NG // 2, NX - 1, NZC, RR, cols // NG), bf16),
            pltpu.VMEM((rounds, NG // 2, NX, NZC, RR, cols // NG), bf16),
            pltpu.VMEM((rounds, NG // 2, NZC - 1, NX, RR, cols // NG), bf16),
            pltpu.VMEM((rounds, NG // 2, NZC, NX, RR, cols // NG), bf16),
            pltpu.VMEM((NG, NX, NZ, NC, NY * panels.shape[0], cols // NG), bf16),
            pltpu.VMEM((NY, panels.shape[0], cols), jnp.float32),
            pltpu.VMEM((NB, RR, cols // NG), bf16),
            pltpu.SMEM((NX * NZC,), jnp.int32),
            pltpu.VMEM((NX, NZC, 8, 128), jnp.int32),
            pltpu.VMEM((NX, NZC, 8, 128), jnp.int32),
            pltpu.VMEM((NZC, NX, 8, 128), jnp.int32),
            dma, dma((rounds,)), dma((rounds,)), dma, dma((rounds, NG // 2)), dma, dma((rounds, NG // 2)),
            dma, dma, dma, dma, dma((2,)), dma((2,)),
            dma((5, NG)), dma, dma((3, NG)), dma((NG,)), dma((2,)), dma((2,)),
        ],
        compiler_params=pltpu.CompilerParams(
            collective_id=0, has_side_effects=True, vmem_limit_bytes=40 * 2**20
        ),
    )(basis.reshape(NY, NB, brows, depth), hbm(panels), hbm(dest))
    out = pl.pallas_call(
        place_kernel,
        out_shape=jax.ShapeDtypeStruct((NB, brows, cols), bf16),
        in_specs=[smem, anywhere],
        out_specs=anywhere,
        scratch_shapes=[dma((NB,))],
        compiler_params=pltpu.CompilerParams(vmem_limit_bytes=2 * 2**20),
    )(table, recv.reshape(NZC * NX, brows, cols))
    return out.reshape(NB * brows, cols)


def solution(mesh):
    in_specs = (P("slab", "store"), P(("slab", "store"), None), P(("slab", "store")))
    out_specs = P(("slab", "store"), None)
    return jax.shard_map(body, mesh=mesh, in_specs=in_specs, out_specs=out_specs, check_vma=False)
```

```python
import functools

import jax
import jax.numpy as jnp
from jax import lax
from jax.experimental import pallas as pl
from jax.experimental.pallas import tpu as pltpu
from jax.sharding import PartitionSpec as P

MESH = pl.DeviceIdType.MESH

NX, NZ, NC, NY = 4, 4, 2, 4
NZC = NZ * NC
NB = 16
RR = 16
AHEAD = 4
HOPS = (1, 3, 2, 0)
HERE = 6
SENT = (0, 1, 2, 3, 4, 5, 7)
NG = 4


def exchange_kernel(
    basis, panels_hbm, dest_hbm, recv, table, panels, dest, arrived, x_out, x_relay, z_out, z_relay, pan, pan_f32, product, pick,
    lab_out, lab_relay, lab_in, a_send, a_recv, a_local, x_send, x_recv, z_send, z_recv, z2_send, z2_recv, x2_send, x2_recv, local, in_sem,
    p_send, py_recv, p_recv, pc_recv, l_send, l_recv,
):
    rounds = arrived.shape[0]
    slab, y = lax.axis_index("slab"), lax.axis_index("store")
    x, zc = slab // NZC, slab % NZC
    z, c = zc // NC, zc % NC

    def at_y(d):
        return (slab, (y + d) % NY)

    def x_of(d):
        return (x + d) % NX

    def at_x(d):
        return (x_of(d) * NZC + zc, y)

    def zc_of(q):
        hop = HOPS[q // NC] if isinstance(q, int) else (q // NC == 0) + 3 * (q // NC == 1) + 2 * (q // NC == 2)
        return (z + hop) % NZ * NC + (c + q) % NC

    def at_zc(q):
        return (x * NZC + zc_of(q), y)

    def at_xz(d, e):
        return (x_of(d) * NZC + zc_of(e * NC), y)

    def remote(src, dst, send, received, device):
        return pltpu.make_async_remote_copy(
            src_ref=src, dst_ref=dst, send_sem=send, recv_sem=received, device_id=device, device_id_type=MESH
        )

    def wait_bytes(ref, sem):
        pltpu.make_async_copy(ref, ref, sem).wait()

    def start_basis(r):
        rows = pl.ds(pl.multiple_of(r * RR, RR), RR)
        for d in (1, 3, 2):
            remote(
                basis.at[(y + d) % NY, :, rows, :], arrived.at[r, y], a_send, a_recv.at[r], at_y(d)
            ).start()
        pltpu.make_async_copy(basis.at[y, :, rows, :], arrived.at[r, y], a_local.at[r]).start()

    panels_in = pltpu.make_async_copy(panels_hbm, panels, in_sem.at[0])
    dest_in = pltpu.make_async_copy(dest_hbm, dest, in_sem.at[1])
    panels_in.start()
    dest_in.start()

    barrier = pltpu.get_barrier_semaphore()
    for d in range(1, NY):
        pl.semaphore_signal(barrier, inc=1, device_id=at_y(d), device_id_type=MESH)
    for d in range(1, NX):
        pl.semaphore_signal(barrier, inc=1, device_id=at_x(d), device_id_type=MESH)
    for d in range(1, NX):
        for e in range(NZ - 1):
            pl.semaphore_signal(barrier, inc=1, device_id=at_xz(d, e), device_id_type=MESH)
    for q in range(NZC):
        if q != HERE:
            pl.semaphore_signal(barrier, inc=1, device_id=at_zc(q), device_id_type=MESH)
    panels_in.wait()
    dest_in.wait()
    pan_f32[y] = panels[...].astype(jnp.float32)
    pl.semaphore_wait(barrier, NY - 1 + NX - 1 + (NX - 1) * (NZ - 1) + NZC - 1)

    for d in range(1, NY):
        remote(pan_f32.at[y], pan_f32.at[y], p_send.at[0, 0], py_recv, at_y(d)).start()
    for r in range(AHEAD):
        start_basis(r)

    width = pan.shape[-1]
    wait_bytes(pan_f32.at[pl.ds(0, NY - 1)], py_recv)
    for g in range(NG):
        part = pan_f32[:, :, g * width : (g + 1) * width]
        pan[g, x, z, c] = part.reshape(pan.shape[4:]).astype(pan.dtype)
        own = pan.at[g, x, z, c]
        for d in (2, 1, 3):
            for e in (2, 0, 1):
                remote(own, own, p_send.at[1, g], p_recv.at[0, g], at_xz(d, e)).start()
            remote(own, own, p_send.at[2, g], p_recv.at[1, g], at_x(d)).start()
        for e in (2, 0, 1):
            remote(own, own, p_send.at[3, g], p_recv.at[2, g], at_zc(e * NC)).start()

    def panels_in_line(g):
        wait_bytes(pan.at[g, pl.ds(0, NX - 1), pl.ds(0, NZ - 1), 0], p_recv.at[0, g])
        wait_bytes(pan.at[g, pl.ds(0, NX - 1), 0, 0], p_recv.at[1, g])
        wait_bytes(pan.at[g, 0, pl.ds(0, NZ - 1), 0], p_recv.at[2, g])
        half = pan.at[g, :, :, c]
        remote(half, half, p_send.at[4, g], pc_recv.at[g], at_zc(HERE + 1)).start()

    def choose(t, _):
        d, q = t // NZC, t % NZC
        target = x_of(d) * NZC + zc_of(q)
        block, place = jnp.int32(0), jnp.int32(-1)
        for b in range(NB):
            value = dest[b]
            hit = value // (NB * NY) == target
            block = jnp.where(hit, b, block)
            place = jnp.where(hit, value % NB, place)
        pick[t] = block
        lab_out[d, q] = jnp.full(lab_out.shape[2:], place, jnp.int32)
        return 0

    lax.fori_loop(0, NX * NZC, choose, 0)

    panels_in_line(0)
    lab_relay[x] = lab_out[0]
    for d in range(1, NX):
        remote(lab_out.at[d], lab_relay.at[x], l_send.at[0], l_recv.at[0], at_x(d)).start()

    def forward(r, g):
        rows, columns = pl.ds(pl.multiple_of(r * RR, RR), RR), pl.ds(g * width, width)
        k = g // 2
        if g % 2 == 0:
            wait_bytes(x_relay.at[r, k, pl.ds(0, NX - 1)], x_recv.at[r, k])
            dst = recv.at[zc, :, rows, columns]
            for q in SENT:
                remote(x_relay.at[r, k, :, q], dst, z2_send, z2_recv, at_zc(q)).start()
            pltpu.make_async_copy(x_relay.at[r, k, :, HERE], dst, local.at[0]).start()
        else:
            wait_bytes(z_relay.at[r, k, pl.ds(0, NZC - 1)], z_recv.at[r, k])
            dst = recv.at[:, x, rows, columns]
            for d in (1, 3, 2):
                remote(z_relay.at[r, k, :, d], dst, x2_send, x2_recv, at_x(d)).start()
            pltpu.make_async_copy(z_relay.at[r, k, :, 0], dst, local.at[1]).start()

    def one_round(r, _):
        @pl.when(r + AHEAD < rounds)
        def _():
            start_basis(r + AHEAD)

        @pl.when(r < rounds)
        def _():
            wait_bytes(arrived.at[r, pl.ds(0, NY - 1)], a_recv.at[r])
            wait_bytes(arrived.at[r, 0], a_local.at[r])
            for g in range(NG):
                @pl.when(r == 0)
                def _():
                    if g + 1 < NG:
                        panels_in_line(g + 1)
                    wait_bytes(pan.at[g, :, :, 0], pc_recv.at[g])

                total = None
                for s in range(NY):
                    left = arrived[r, s].reshape(NB * RR, arrived.shape[-1])
                    right = pan[g, s].reshape(arrived.shape[-1], width)
                    term = jnp.dot(left, right, preferred_element_type=jnp.float32)
                    total = term if total is None else total + term
                product[...] = total.astype(product.dtype).reshape(product.shape)
                k = g // 2
                if g % 2 == 0:
                    for d in range(1, NX):
                        for q in range(NZC):
                            x_out[r, k, d - 1, q] = product[pick[d * NZC + q]]
                    for d in (1, 3, 2):
                        remote(
                            x_out.at[r, k, d - 1], x_relay.at[r, k, x], x_send, x_recv.at[r, k], at_x(d)
                        ).start()
                    for q in range(NZC):
                        x_relay[r, k, x, q] = product[pick[q]]
                else:
                    for q in range(NZC):
                        for d in range(NX):
                            if q == HERE:
                                z_relay[r, k, zc, d] = product[pick[d * NZC + q]]
                            else:
                                z_out[r, k, SENT.index(q), d] = product[pick[d * NZC + q]]
                    for i, q in enumerate(SENT):
                        remote(
                            z_out.at[r, k, i], z_relay.at[r, k, zc], z_send, z_recv.at[r, k], at_zc(q)
                        ).start()

        @pl.when(r >= 1)
        def _():
            for g in range(NG):
                forward(r - 1, g)

        @pl.when(r == 1)
        def _():
            wait_bytes(lab_relay.at[pl.ds(0, NX - 1)], l_recv.at[0])
            for q in range(NZC):
                if q != HERE:
                    remote(lab_relay.at[:, q], lab_in.at[zc], l_send.at[1], l_recv.at[1], at_zc(q)).start()
            lab_in[zc] = lab_relay[:, HERE]

        @pl.when(r == 3)
        def _():
            wait_bytes(lab_in.at[pl.ds(0, NZC - 1)], l_recv.at[1])
            lane = lax.broadcasted_iota(jnp.int32, table.shape, 1)
            places = jnp.zeros(table.shape, jnp.int32)
            for q in range(NZC):
                for s in range(NX):
                    places = jnp.where(lane == q * NX + s, lab_in[q, s], places)
            table[...] = places

        return 0

    lax.fori_loop(0, rounds + 1, one_round, 0)

    wait_bytes(pan_f32.at[pl.ds(0, NY - 1)], p_send.at[0, 0])
    for g in range(NG):
        wait_bytes(pan.at[g, pl.ds(0, NX - 1), pl.ds(0, NZ - 1), 0], p_send.at[1, g])
        wait_bytes(pan.at[g, pl.ds(0, NX - 1), 0, 0], p_send.at[2, g])
        wait_bytes(pan.at[g, 0, pl.ds(0, NZ - 1), 0], p_send.at[3, g])
        wait_bytes(pan.at[g, :, :, 0], p_send.at[4, g])
    wait_bytes(lab_relay.at[pl.ds(0, NX - 1)], l_send.at[0])
    wait_bytes(lab_in.at[pl.ds(0, NZC - 1)], l_send.at[1])
    wait_bytes(arrived.at[:, pl.ds(0, NY - 1)], a_send)
    wait_bytes(x_out, x_send)
    half = pl.ds(0, NG // 2 * width)
    wait_bytes(z_out, z_send)
    wait_bytes(recv.at[0, :, :, half], local.at[0])
    wait_bytes(recv.at[:, 0, :, half], local.at[1])
    wait_bytes(recv.at[pl.ds(0, NZC - 1), :, :, half], z2_send)
    wait_bytes(recv.at[:, pl.ds(0, NX - 1), :, half], x2_send)
    wait_bytes(recv.at[pl.ds(0, NZC - 1), :, :, half], z2_recv)
    wait_bytes(recv.at[:, pl.ds(0, NX - 1), :, half], x2_recv)


def place_kernel(table, recv, out, sem):
    for s in range(recv.shape[0]):
        place = table[0, s]

        @pl.when(place >= 0)
        def _():
            pltpu.make_async_copy(recv.at[s], out.at[place], sem.at[place]).start()

    for p in range(NB):
        pltpu.make_async_copy(recv.at[0], out.at[p], sem.at[p]).wait()


def body(basis, panels, dest):
    depth = basis.shape[1]
    cols = panels.shape[1]
    brows = basis.shape[0] // (NY * NB)
    rounds = brows // RR
    bf16 = basis.dtype
    anywhere = pl.BlockSpec(memory_space=pl.ANY)
    vmem = pl.BlockSpec(memory_space=pltpu.VMEM)
    smem = pl.BlockSpec(memory_space=pltpu.SMEM)
    in_hbm = pl.BlockSpec(memory_space=pltpu.HBM)
    hbm = lambda a: pltpu.with_memory_space_constraint(a, pltpu.HBM)
    dma = pltpu.SemaphoreType.DMA
    recv, table = pl.pallas_call(
        exchange_kernel,
        out_shape=(
            jax.ShapeDtypeStruct((NZC, NX, brows, cols), bf16),
            jax.ShapeDtypeStruct((1, 128), jnp.int32),
        ),
        in_specs=[anywhere, in_hbm, in_hbm],
        out_specs=(anywhere, vmem),
        scratch_shapes=[
            pltpu.VMEM(panels.shape, bf16),
            pltpu.SMEM(dest.shape, jnp.int32),
            pltpu.VMEM((rounds, NY, NB, RR, depth), bf16),
            pltpu.VMEM((rounds, NG // 2, NX - 1, NZC, RR, cols // NG), bf16),
            pltpu.VMEM((rounds, NG // 2, NX, NZC, RR, cols // NG), bf16),
            pltpu.VMEM((rounds, NG // 2, NZC - 1, NX, RR, cols // NG), bf16),
            pltpu.VMEM((rounds, NG // 2, NZC, NX, RR, cols // NG), bf16),
            pltpu.VMEM((NG, NX, NZ, NC, NY * panels.shape[0], cols // NG), bf16),
            pltpu.VMEM((NY, panels.shape[0], cols), jnp.float32),
            pltpu.VMEM((NB, RR, cols // NG), bf16),
            pltpu.SMEM((NX * NZC,), jnp.int32),
            pltpu.VMEM((NX, NZC, 1, 128), jnp.int32),
            pltpu.VMEM((NX, NZC, 1, 128), jnp.int32),
            pltpu.VMEM((NZC, NX, 1, 128), jnp.int32),
            dma, dma((rounds,)), dma((rounds,)), dma, dma((rounds, NG // 2)), dma, dma((rounds, NG // 2)),
            dma, dma, dma, dma, dma((2,)), dma((2,)),
            dma((5, NG)), dma, dma((3, NG)), dma((NG,)), dma((2,)), dma((2,)),
        ],
        compiler_params=pltpu.CompilerParams(
            collective_id=0, has_side_effects=True, vmem_limit_bytes=40 * 2**20
        ),
    )(basis.reshape(NY, NB, brows, depth), hbm(panels), hbm(dest))
    out = pl.pallas_call(
        place_kernel,
        out_shape=jax.ShapeDtypeStruct((NB, brows, cols), bf16),
        in_specs=[smem, anywhere],
        out_specs=anywhere,
        scratch_shapes=[dma((NB,))],
        compiler_params=pltpu.CompilerParams(vmem_limit_bytes=2 * 2**20),
    )(table, recv.reshape(NZC * NX, brows, cols))
    return out.reshape(NB * brows, cols)


def solution(mesh):
    in_specs = (P("slab", "store"), P(("slab", "store"), None), P(("slab", "store")))
    out_specs = P(("slab", "store"), None)
    return jax.shard_map(body, mesh=mesh, in_specs=in_specs, out_specs=out_specs, check_vma=False)
```
